128 devices in a mesh: dp: 2 (over y_hi), ctx: 32 (over x, y_lo, z), head: 2 (over core).
Axes of the slice: x: 4, y: 4 (y_hi: 2, y_lo: 2; y = y_hi * 2 + y_lo), z: 4, core: 2. Of those that a mesh axis runs over, the one named last changes fastest.
Arguments:
- tokens: bfloat16 [16384, 768], P(('dp', 'ctx', 'head')), may hold values from -6 to 6
- first_gain: bfloat16 [768], P(('dp', 'ctx', 'head')), may hold values from 0.099609375 to 1.8984375
- first_shift: bfloat16 [768], P(('dp', 'ctx', 'head')), may hold values from -3 to 3
- second_gain: bfloat16 [768], P(('dp', 'ctx', 'head')), may hold values from 0.099609375 to 1.8984375
- second_shift: bfloat16 [768], P(('dp', 'ctx', 'head')), may hold values from -3 to 3
- qkv_weight: bfloat16 [768, 2304], P(('dp', 'ctx', 'head')), may hold values from -0.21875 to 0.21875
- out_weight: bfloat16 [768, 768], P(('dp', 'ctx', 'head')), may hold values from -0.875 to 0.875
- up_weight: bfloat16 [768, 3072], P(('dp', 'ctx', 'head')), may hold values from -0.21875 to 0.21875
- down_weight: bfloat16 [3072, 768], P(('dp', 'ctx', 'head')), may hold values from -0.109375 to 0.109375
- cotangent: bfloat16 [16384, 768], P(('dp', 'ctx', 'head')), may hold values from -6 to 6
Outputs:
- layer_out: bfloat16 [16384, 768], P(('dp', 'ctx', 'head'))
- tokens_grad: bfloat16 [16384, 768], P(('dp', 'ctx', 'head'))
- first_gain_grad: float32 [768], P(('dp', 'ctx', 'head'))
- first_shift_grad: float32 [768], P(('dp', 'ctx', 'head'))
- second_gain_grad: float32 [768], P(('dp', 'ctx', 'head'))
- second_shift_grad: float32 [768], P(('dp', 'ctx', 'head'))
- qkv_grad: float32 [768, 2304], P(('dp', 'ctx', 'head'))
- out_grad: float32 [768, 768], P(('dp', 'ctx', 'head'))
- up_grad: float32 [768, 3072], P(('dp', 'ctx', 'head'))
- down_grad: float32 [3072, 768], P(('dp', 'ctx', 'head'))
The draws below stay inside these ranges and needn't reach their ends.
All inputs are finite; a program needn't handle non-finite values.
Results may differ from the reference program's by a relative error of at most 0.015.
Values may be sent and summed in bfloat16 or wider, within the bound.
No kernel may reach another device: no remote copies, remote signals or barrier semaphores. Data moves between devices by JAX's collectives and lax.ppermute only.
A program may use at most 256 MiB of HBM per device.

```python
import jax
import jax.numpy as jnp
from jax import lax

D = 768
H = 12
HS = 64
ROT = 16
FF = 3072
LEN = 8192
TOKENS = 16384
N_DP = 2


def block_levels(key, shape, pieces, low, largest):
    loudness = 1.0
    for position, parts in pieces:
        heights = jax.random.uniform(jax.random.fold_in(jax.random.fold_in(key, 6), position), (parts,), jnp.float32, low / len(pieces), largest / len(pieces))
        loudness = loudness * jnp.repeat(jnp.exp(heights), shape[position] // parts).reshape((-1,) + (1,) * (len(shape) - 1 - position))
    return loudness


def normal_values(own_key, shape, deviation, bound, shards=(), kind=jnp.bfloat16):
    loudness = block_levels(own_key, shape, shards, -0.22, 0.18) if shards else 1.0
    values = jax.random.normal(own_key, shape, jnp.float32) * deviation * loudness
    return jnp.minimum(jnp.maximum(values, -bound), bound).astype(kind)


def setup_inputs(seed: int = 0) -> dict:
    keys = jax.random.split(jax.random.key(seed), 11)
    return {
        "tokens": normal_values(keys[0], (TOKENS, D), 1.0, 6.0, ((0, 128),)),
        "first_gain": jnp.clip(1.0 + 0.18 * jax.random.normal(keys[1], (D,), jnp.float32), 0.099609375, 1.8984375).astype(jnp.bfloat16),
        "first_shift": normal_values(keys[2], (D,), 0.3, 3.0, ((0, 128),)),
        "second_gain": jnp.clip(1.0 + 0.18 * jax.random.normal(keys[3], (D,), jnp.float32), 0.099609375, 1.8984375).astype(jnp.bfloat16),
        "second_shift": normal_values(keys[4], (D,), 0.3, 3.0, ((0, 128),)),
        "qkv_weight": normal_values(keys[5], (D, 3 * D), D ** -0.5, 0.21875, ((0, 128),)),
        "out_weight": normal_values(keys[6], (D, D), (D // 16) ** -0.5, 0.875, ((0, 128),)),
        "up_weight": normal_values(keys[7], (D, FF), D ** -0.5, 0.21875, ((0, 128),)),
        "down_weight": normal_values(keys[8], (FF, D), FF ** -0.5, 0.109375, ((0, 128),)),
        "cotangent": normal_values(keys[9], (TOKENS, D), 1.0, 6.0, ((0, 128),)),
    }


EPSILON = 1e-05

@jax.custom_vjp
def low(v):
    return lax.optimization_barrier(v.astype(jnp.bfloat16)).astype(jnp.float32)

@jax.custom_vjp
def low_back(v):
    return v

def low_keep(v):
    return (low(v), None)

def low_pass(kept, grad):
    return (grad,)

def back_keep(v):
    return (v, None)

def back_low(kept, grad):
    return (low(grad),)
low.defvjp(low_keep, low_pass)
low_back.defvjp(back_keep, back_low)

def matmul(left, right):
    return jnp.dot(left, right, precision=lax.Precision.HIGHEST, preferred_element_type=jnp.float32)

def layer_norm(values, gain_vec, shift_vec):
    middle = lax.optimization_barrier(jnp.mean(values, axis=-1, keepdims=True))
    centred = values - middle
    spread = lax.optimization_barrier(jnp.mean(centred * centred, axis=-1, keepdims=True))
    return centred * lax.rsqrt(spread + EPSILON) * gain_vec + shift_vec

def rotary_tables(positions, rot_dims):
    inverse = 1.0 / 10000.0 ** (jnp.arange(0, rot_dims, 2, dtype=jnp.float32) / rot_dims)
    angles = positions.astype(jnp.float32)[:, None] * inverse[None, :]
    angles = jnp.concatenate([angles, angles], axis=1)
    return (jnp.cos(angles), jnp.sin(angles))

def rotate_heads(values, cosine, sine_vals):
    half_dims = ROT // 2
    rotated_part = values[..., :ROT]
    turned_half = jnp.concatenate([-rotated_part[..., half_dims:], rotated_part[..., :half_dims]], axis=-1)
    mixed = rotated_part * cosine[:, None, :] + turned_half * sine_vals[:, None, :]
    return jnp.concatenate([mixed, values[..., ROT:]], axis=-1)

def attention(queries, keys_all, values_all):
    seq_length = queries.shape[1]
    query_block = min(512, seq_length)
    key_places = jnp.arange(seq_length, dtype=jnp.int32)

    def one_block(block_index):
        query_rows = lax.dynamic_slice_in_dim(queries, block_index * query_block, query_block, 1)
        scores = jnp.einsum('hqd,hkd->hqk', query_rows, keys_all, precision=lax.Precision.HIGHEST) * HS ** (-0.5)
        scores = low_back(scores)
        query_places = block_index * query_block + jnp.arange(query_block, dtype=jnp.int32)
        visible = key_places[None, :] <= query_places[:, None]
        scores = jnp.where(visible[None], scores, -1e+30)
        row_top = lax.optimization_barrier(jnp.max(scores, axis=-1, keepdims=True))
        weights = jnp.exp(scores - row_top)
        weights = weights / lax.optimization_barrier(jnp.sum(weights, axis=-1, keepdims=True))
        return jnp.einsum('hqk,hkd->hqd', low(weights), values_all, precision=lax.Precision.HIGHEST)
    outputs = lax.map(jax.checkpoint(one_block), jnp.arange(seq_length // query_block, dtype=jnp.int32))
    return jnp.transpose(outputs, (1, 0, 2, 3)).reshape(queries.shape[0], seq_length, HS)

def sequence_layer(seq_rows, params):
    first_gain, first_shift, second_gain, second_shift, qkv_weight, out_weight, up_weight, down_weight = params
    seq_length = seq_rows.shape[0]
    first_low = low(layer_norm(seq_rows, first_gain, first_shift))
    second_low = low(layer_norm(seq_rows, second_gain, second_shift))
    projected = low_back(matmul(first_low, qkv_weight)).reshape(seq_length, H, 3, HS)
    cosine, sine_vals = rotary_tables(jnp.arange(seq_length, dtype=jnp.int32), ROT)
    queries = low_back(low(rotate_heads(projected[:, :, 0], cosine, sine_vals)))
    keys_all = low_back(low(rotate_heads(projected[:, :, 1], cosine, sine_vals)))
    values_all = low_back(low(projected[:, :, 2]))
    heads_out = attention(jnp.transpose(queries, (1, 0, 2)), jnp.transpose(keys_all, (1, 0, 2)), jnp.transpose(values_all, (1, 0, 2)))
    heads_low = low_back(low(jnp.transpose(heads_out, (1, 0, 2)).reshape(seq_length, H * HS)))
    attended = matmul(heads_low, out_weight)
    hidden = low_back(matmul(second_low, up_weight))
    activated = low(jax.nn.gelu(hidden, approximate=False))
    return seq_rows + attended + matmul(activated, down_weight)

def reference(tokens, first_gain, first_shift, second_gain, second_shift, qkv_weight, out_weight, up_weight, down_weight, cotangent):
    params = tuple((member.astype(jnp.float32) for member in (first_gain, first_shift, second_gain, second_shift, qkv_weight, out_weight, up_weight, down_weight)))
    rows_all = tokens.astype(jnp.float32).reshape(N_DP, LEN, D)
    cot_all = cotangent.astype(jnp.float32).reshape(N_DP, LEN, D)

    def per_sequence(grad_sums, seq_pair):
        seq_rows, seq_cot = seq_pair
        result, pullback = jax.vjp(sequence_layer, seq_rows, params)
        row_grad, param_grads = pullback(seq_cot)
        grad_sums = jax.tree.map(jnp.add, grad_sums, param_grads)
        return (grad_sums, (result, row_grad))
    zero_sums = jax.tree.map(jnp.zeros_like, params)
    grads, (results, row_grads) = lax.scan(per_sequence, zero_sums, (rows_all, cot_all))
    layer_out = results.reshape(TOKENS, D).astype(jnp.bfloat16)
    tokens_grad = row_grads.reshape(TOKENS, D).astype(jnp.bfloat16)
    return (layer_out, tokens_grad, grads[0], grads[1], grads[2], grads[3], grads[4], grads[5], grads[6], grads[7])
```

```python
import functools

import jax
import jax.numpy as jnp
from jax import lax
from jax.experimental import pallas as pl
from jax.experimental.pallas import tpu as pltpu
from jax.sharding import Mesh, PartitionSpec as P

H = 12
HS = 64
ROT = 16
D = 768
FF = 3072
EPSILON = 1e-05
BF = jnp.bfloat16
F32 = jnp.float32
CHIPS = ("dp", "x", "y", "z")
ALL = ("dp", "x", "y", "z", "c")
GH = 3
QN = 512
NB = 16


def layer_norm(values, gain_vec, shift_vec):
    middle = jnp.mean(values, axis=-1, keepdims=True)
    centred = values - middle
    spread = jnp.mean(centred * centred, axis=-1, keepdims=True)
    return centred * lax.rsqrt(spread + EPSILON) * gain_vec + shift_vec


def exact_gelu(values):
    return jax.nn.gelu(values, approximate=False)


def dot(a, b, dims=((1,), (0,))):
    return lax.dot_general(a, b, (dims, ((), ())), preferred_element_type=F32)


def attn_kernel(qd_ref, kv_ref, oq_ref, dkv_ref, kt_ref):
    x = lax.axis_index("x")
    z = lax.axis_index("z")
    qd = qd_ref[...]
    lane = lax.broadcasted_iota(jnp.int32, (QN, 128), 1)
    zero = jnp.zeros_like(qd)
    q0 = jnp.where(lane < HS, qd, zero)
    do0 = jnp.where(lane >= HS, qd, zero)
    q_t = q0.astype(F32).T.astype(BF)
    do_f = do0.astype(F32).T
    do_t = do_f.astype(BF)
    col = lax.broadcasted_iota(jnp.int32, (1, QN), 1)
    q_place = (col // 256) * 1024 + z * 256 + col % 256
    krow = lax.broadcasted_iota(jnp.int32, (QN, 1), 0)
    k_place = (krow // 256) * 1024 + krow % 256

    def fwd(b, carry, masked):
        m, l, acc = carry
        start = pl.multiple_of(b * QN, QN)
        k = kv_ref[pl.ds(start, QN), :]
        k_t = k.astype(F32).T.astype(BF)
        kt_ref[b] = k_t
        s = dot(k, q_t)
        if masked:
            s = jnp.where(k_place + (b % 4) * 256 <= q_place, s, -1e30)
        m_new = jnp.maximum(m, jnp.max(s, axis=0, keepdims=True))
        p = jnp.exp(s - m_new)
        alpha = jnp.exp(m - m_new)
        l = l * alpha + jnp.sum(p, axis=0, keepdims=True)
        acc = acc * alpha + dot(k_t, p.astype(BF))
        return m_new, l, acc

    carry = (
        jnp.full((1, QN), -1e30, F32),
        jnp.zeros((1, QN), F32),
        jnp.zeros((128, QN), F32),
    )
    carry = lax.fori_loop(0, 4 * x, functools.partial(fwd, masked=False), carry)
    m, l, acc = lax.fori_loop(4 * x, 4 * x + 4, functools.partial(fwd, masked=True), carry)
    lse = m + jnp.log(l)
    o_low = (acc / l).astype(BF).astype(F32)
    delta = jnp.sum(do_f * o_low, axis=0, keepdims=True)

    def bwd(b, dq, masked):
        start = pl.multiple_of(b * QN, QN)
        k = kv_ref[pl.ds(start, QN), :]
        s = dot(k, q_t)
        p = jnp.exp(s - lse)
        if masked:
            p = jnp.where(k_place + (b % 4) * 256 <= q_place, p, 0.0)
        dp = dot(k, do_t)
        ds = (p * (dp - delta)).astype(BF)
        dkv_ref[pl.ds(start, QN), :] = (dot(ds, q0) + dot(p.astype(BF), do0)).astype(BF)
        return dq + dot(kt_ref[b], ds)

    dq = jnp.zeros((128, QN), F32)
    dq = lax.fori_loop(0, 4 * x, functools.partial(bwd, masked=False), dq)
    dq = lax.fori_loop(4 * x, 4 * x + 4, functools.partial(bwd, masked=True), dq)

    def blank(b, _):
        dkv_ref[pl.ds(pl.multiple_of(b * QN, QN), QN), :] = jnp.zeros((QN, 128), BF)
        return 0

    lax.fori_loop(4 * x + 4, NB, blank, 0)
    row = lax.broadcasted_iota(jnp.int32, (128, QN), 0)
    oq_ref[...] = jnp.where(row < HS, dq * HS ** (-0.5), o_low).T.astype(BF)


def attention(qd, kv):
    return pl.pallas_call(
        attn_kernel,
        grid=(GH,),
        in_specs=[
            pl.BlockSpec((QN, 128), lambda h: (0, h)),
            pl.BlockSpec((NB * QN, 128), lambda h: (0, h)),
        ],
        out_specs=[
            pl.BlockSpec((QN, 128), lambda h: (0, h)),
            pl.BlockSpec((NB * QN, 128), lambda h: (0, h)),
        ],
        out_shape=[
            jax.ShapeDtypeStruct((QN, GH * 128), BF),
            jax.ShapeDtypeStruct((NB * QN, GH * 128), BF),
        ],
        scratch_shapes=[pltpu.VMEM((NB, 128, QN), BF)],
        compiler_params=pltpu.CompilerParams(vmem_limit_bytes=50 * 1024 * 1024),
        cost_estimate=pl.CostEstimate(
            flops=3 * 7 * 2 * 512 * 8192 * 128, bytes_accessed=14000000, transcendentals=3 * 2 * 512 * 8192
        ),
    )(qd, kv)


def swap_cores(v):
    return lax.ppermute(v, "c", [(0, 1), (1, 0)])


def gather_packed(packed):
    mine = lax.all_to_all(jnp.broadcast_to(packed[None], (64,) + packed.shape), CHIPS, 0, 0)
    return mine, swap_cores(mine)


def scatter_sum(own_half, other_half):
    got = swap_cores(other_half)
    chip = (own_half.astype(F32) + got.astype(F32)).astype(BF)
    parts = lax.all_to_all(chip, CHIPS, 0, 0)
    return jnp.sum(parts.astype(F32), axis=0)


def halves(grad, width):
    rows = 6 * width // 128
    g = grad.reshape(2, 64, rows, 128)
    return g[0], g[1]


def local(
    tokens,
    first_gain,
    first_shift,
    second_gain,
    second_shift,
    qkv_weight,
    out_weight,
    up_weight,
    down_weight,
    cotangent,
):
    x = lax.axis_index("x")
    y = lax.axis_index("y")
    z = lax.axis_index("z")
    c = lax.axis_index("c")

    vecs = jnp.concatenate([first_gain, first_shift, second_gain, second_shift])
    vec_row = jnp.pad(vecs, (0, 16 * 128 - 24)).reshape(16, 128)
    pack_one = jnp.concatenate(
        [qkv_weight.reshape(108, 128), out_weight.reshape(36, 128), vec_row], axis=0
    )
    pack_two = jnp.concatenate([up_weight.reshape(144, 128), down_weight.reshape(144, 128)], axis=0)

    one_a, one_b = gather_packed(pack_one)

    def both(a, b, lo, hi):
        return jnp.stack([a[:, lo:hi], b[:, lo:hi]])

    qkv_full = both(one_a, one_b, 0, 108).reshape(D, 3 * D)
    out_full = both(one_a, one_b, 108, 144).reshape(D, D)
    vec_full = both(one_a, one_b, 144, 145)[:, :, 0, :24].reshape(2, 64, 4, 6)
    vec_full = jnp.transpose(vec_full, (2, 0, 1, 3)).reshape(4, D).astype(F32)

    place = jnp.arange(D, dtype=jnp.int32)
    core = jnp.where(place < D // 2, c, 1 - c)
    source = (place % (D // 2)) // 6 * 12 + core * 6 + place % 6
    perm = (jnp.arange(D, dtype=jnp.int32)[:, None] == source[None, :]).astype(BF)

    def to_gathered(v):
        return dot(v, perm).astype(BF)

    def from_gathered(v):
        return dot(v, perm, ((1,), (1,))).astype(BF)

    rows_f32 = to_gathered(tokens).astype(F32)
    cot_f32 = to_gathered(cotangent).astype(F32)
    first_norm, first_pull = jax.vjp(layer_norm, rows_f32, vec_full[0], vec_full[1])
    second_norm, second_pull = jax.vjp(layer_norm, rows_f32, vec_full[2], vec_full[3])
    first_low = first_norm.astype(BF)
    second_low = second_norm.astype(BF)

    row_first = (x * 8 + y * 4 + z) * 256 + c * 128
    lane = jnp.arange(3 * HS, dtype=jnp.int32)
    entry = lane % HS
    turned_lane = (entry < ROT) & (lane < 2 * HS)
    inverse = 1.0 / 10000.0 ** (2.0 * (entry % 8).astype(F32) / ROT)
    angles = (row_first + jnp.arange(128, dtype=jnp.int32)).astype(F32)[:, None] * inverse[None, :]
    cos_t = jnp.where(turned_lane, jnp.cos(angles), 1.0)
    sin_t = jnp.where(turned_lane, jnp.sin(angles), 0.0)
    sin_lo = jnp.where(entry < 8, sin_t, 0.0)
    sin_hi = jnp.where(entry >= 8, sin_t, 0.0)

    def rotate(v, sign):
        v = v.reshape(128, H, 3 * HS)
        ahead = jnp.roll(v, -8, axis=2)
        behind = jnp.roll(v, 8, axis=2)
        return v * cos_t[:, None] + sign * (behind * sin_hi[:, None] - ahead * sin_lo[:, None])

    turned = rotate(dot(first_low, qkv_full), 1.0)
    heads_grad = from_gathered(dot(cotangent, out_full, ((1,), (1,))).astype(BF))
    query = (turned[:, :, :HS] * HS ** (-0.5)).astype(BF)
    key_val = turned[:, :, HS:].astype(BF)
    query_grad_pair = jnp.concatenate([query, heads_grad.reshape(128, H, HS)], axis=2)
    send = jnp.concatenate(
        [query_grad_pair.reshape(128, 4, GH * 128), key_val.reshape(128, 4, GH * 128)], axis=2
    )
    got = lax.all_to_all(jnp.transpose(send, (1, 0, 2)), ("y", "c"), 0, 0).reshape(QN, 2 * GH * 128)
    qd = got[:, : GH * 128]
    kv = lax.all_gather(got[:, GH * 128 :], ("x", "z"), axis=0, tiled=True)

    two_a, two_b = gather_packed(pack_two)
    up_full = both(two_a, two_b, 0, 144).reshape(D, FF)
    down_a = two_a[:, 144:].reshape(64, 24, D)
    down_b = two_b[:, 144:].reshape(64, 24, D)
    down_full = jnp.stack(
        [jnp.where(c == 0, down_a, down_b), jnp.where(c == 0, down_b, down_a)], axis=1
    ).reshape(FF, D)
    hidden = dot(second_low, up_full)
    activated, gelu_pull = jax.vjp(exact_gelu, hidden)
    act_low = activated.astype(BF)
    feed_out = dot(act_low, down_full)
    act_grad = dot(cotangent, down_full, ((1,), (1,)))
    (hidden_grad,) = gelu_pull(act_grad)
    hidden_low = hidden_grad.astype(BF)
    up_w_grad = dot(second_low, hidden_low, ((0,), (0,))).astype(BF)
    down_w_grad = dot(act_low, cotangent, ((0,), (0,))).astype(BF)
    second_in = dot(hidden_low, up_full, ((1,), (1,)))
    second_rows, gain_two_grad, shift_two_grad = second_pull(second_in)

    oq, dkv = attention(qd, kv)
    oq = oq.reshape(QN, GH, 2, HS)
    dkv_mine = lax.psum_scatter(dkv, ("x", "z"), scatter_dimension=0, tiled=True)

    up_own, up_other = halves(up_w_grad, FF)
    down_g = down_w_grad.reshape(64, 2, 24, D)
    down_own = jnp.where(c == 0, down_g[:, 0], down_g[:, 1]).reshape(64, 144, 128)
    down_other = jnp.where(c == 0, down_g[:, 1], down_g[:, 0]).reshape(64, 144, 128)
    two_sum = scatter_sum(
        jnp.concatenate([up_own, down_own], axis=1), jnp.concatenate([up_other, down_other], axis=1)
    )
    up_out = two_sum[:144].reshape(6, FF)
    down_out = two_sum[144:].reshape(24, D)

    token_heads = lax.all_to_all(oq[:, :, 1].reshape(4, 128, GH * HS), ("y", "c"), 0, 0)
    token_heads = to_gathered(jnp.transpose(token_heads, (1, 0, 2)).reshape(128, D))
    attended = dot(token_heads, out_full)
    layer_out = (tokens.astype(F32) + attended + feed_out).astype(BF)
    out_w_grad = dot(token_heads, cotangent, ((0,), (0,))).astype(BF)

    assembled = jnp.concatenate(
        [oq[:, :, 0], dkv_mine.reshape(QN, GH, 2 * HS)], axis=2
    ).reshape(4, 128, GH * 3 * HS)
    back = lax.all_to_all(assembled, ("y", "c"), 0, 0)
    back = jnp.transpose(back, (1, 0, 2)).reshape(128, 3 * D)
    pre_low = rotate(back.astype(F32), -1.0).astype(BF).reshape(128, 3 * D)
    qkv_w_grad = dot(first_low, pre_low, ((0,), (0,))).astype(BF)
    first_in = dot(pre_low, qkv_full, ((1,), (1,)))
    first_rows, gain_one_grad, shift_one_grad = first_pull(first_in)
    tokens_grad = from_gathered((cot_f32 + first_rows + second_rows).astype(BF))

    vec_grad = jnp.stack([gain_one_grad, shift_one_grad, gain_two_grad, shift_two_grad]).astype(BF)
    vec_grad = jnp.transpose(vec_grad.reshape(4, 2, 64, 6), (1, 2, 0, 3)).reshape(2, 64, 24)
    vec_grad = jnp.pad(vec_grad, ((0, 0), (0, 0), (0, 16 * 128 - 24))).reshape(2, 64, 16, 128)
    qkv_own, qkv_other = halves(qkv_w_grad, 3 * D)
    out_own, out_other = halves(out_w_grad, D)
    one_sum = scatter_sum(
        jnp.concatenate([qkv_own, out_own, vec_grad[0]], axis=1),
        jnp.concatenate([qkv_other, out_other, vec_grad[1]], axis=1),
    )
    qkv_out = one_sum[:108].reshape(6, 3 * D)
    out_out = one_sum[108:144].reshape(6, D)
    vec_out = one_sum[144, :24].reshape(4, 6)
    return (
        layer_out,
        tokens_grad,
        vec_out[0],
        vec_out[1],
        vec_out[2],
        vec_out[3],
        qkv_out,
        out_out,
        up_out,
        down_out,
    )


def solution(mesh):
    fine = Mesh(mesh.devices.reshape(2, 4, 2, 4, 2), ALL)
    rows = P(ALL, None)
    vec = P(ALL)
    in_specs = (rows, vec, vec, vec, vec, rows, rows, rows, rows, rows)
    out_specs = (rows, rows, vec, vec, vec, vec, rows, rows, rows, rows)
    return jax.shard_map(local, mesh=fine, in_specs=in_specs, out_specs=out_specs, check_vma=False)
```

```python
import functools

import jax
import jax.numpy as jnp
from jax import lax
from jax.experimental import pallas as pl
from jax.experimental.pallas import tpu as pltpu
from jax.sharding import Mesh, PartitionSpec as P

H = 12
HS = 64
ROT = 16
D = 768
FF = 3072
EPSILON = 1e-05
BF = jnp.bfloat16
F32 = jnp.float32
CHIPS = ("dp", "x", "y", "z")
ALL = ("dp", "x", "y", "z", "c")
GH = 3
QN = 512


def layer_norm(values, gain_vec, shift_vec):
    middle = jnp.mean(values, axis=-1, keepdims=True)
    centred = values - middle
    spread = jnp.mean(centred * centred, axis=-1, keepdims=True)
    return centred * lax.rsqrt(spread + EPSILON) * gain_vec + shift_vec


def exact_gelu(values):
    return jax.nn.gelu(values, approximate=False)


def dot(a, b, dims=((1,), (0,))):
    return lax.dot_general(a, b, (dims, ((), ())), preferred_element_type=F32)


def attn_kernel(qd_ref, *refs):
    kv_refs, oq_ref, d_refs, kt_ref = refs[:4], refs[4], refs[5:9], refs[9]
    x = lax.axis_index("x")
    z = lax.axis_index("z")
    qd = qd_ref[...]
    lane = lax.broadcasted_iota(jnp.int32, (QN, 128), 1)
    zero = jnp.zeros_like(qd)
    q0 = jnp.where(lane < HS, qd, zero)
    do0 = jnp.where(lane >= HS, qd, zero)
    q_t = q0.astype(F32).T.astype(BF)
    do_f = do0.astype(F32).T
    do_t = do_f.astype(BF)
    col = lax.broadcasted_iota(jnp.int32, (1, QN), 1)
    q_place = (col // 256) * 1024 + z * 256 + col % 256
    krow = lax.broadcasted_iota(jnp.int32, (QN, 1), 0)
    k_place = (krow // 256) * 1024 + krow % 256

    def visible(i):
        return k_place + ((z - i + 4) % 4) * 256 <= q_place

    def fwd(i, carry, slab):
        m, l, acc = carry
        k = kv_refs[slab][i]
        k_t = k.astype(F32).T.astype(BF)
        kt_ref[slab, i] = k_t
        s = dot(k, q_t)
        if slab == 0:
            s = jnp.where(visible(i), s, -1e30)
        m_new = jnp.maximum(m, jnp.max(s, axis=0, keepdims=True))
        p = jnp.exp(s - m_new)
        alpha = jnp.exp(m - m_new)
        l = l * alpha + jnp.sum(p, axis=0, keepdims=True)
        acc = acc * alpha + dot(k_t, p.astype(BF))
        return m_new, l, acc

    carry = (
        jnp.full((1, QN), -1e30, F32),
        jnp.zeros((1, QN), F32),
        jnp.zeros((128, QN), F32),
    )
    for slab in range(4):
        count = jnp.where(x >= slab, 4, 0)
        carry = lax.fori_loop(0, count, functools.partial(fwd, slab=slab), carry)
    m, l, acc = carry
    lse = m + jnp.log(l)
    o_low = (acc / l).astype(BF).astype(F32)
    delta = jnp.sum(do_f * o_low, axis=0, keepdims=True)

    def bwd(i, dq, slab):
        k = kv_refs[slab][i]
        s = dot(k, q_t)
        p = jnp.exp(s - lse)
        if slab == 0:
            p = jnp.where(visible(i), p, 0.0)
        dp = dot(k, do_t)
        ds = (p * (dp - delta)).astype(BF)
        d_refs[slab][i] = (dot(ds, q0) + dot(p.astype(BF), do0)).astype(BF)
        return dq + dot(kt_ref[slab, i], ds)

    dq = jnp.zeros((128, QN), F32)
    for slab in range(4):
        count = jnp.where(x >= slab, 4, 0)
        dq = lax.fori_loop(0, count, functools.partial(bwd, slab=slab), dq)
        if slab > 0:

            @pl.when(x < slab)
            def _():
                d_refs[slab][...] = jnp.zeros((4, QN, 128), BF)

    row = lax.broadcasted_iota(jnp.int32, (128, QN), 0)
    oq_ref[...] = jnp.where(row < HS, dq * HS ** (-0.5), o_low).T.astype(BF)


def attention(qd, kvs):
    slab = jax.ShapeDtypeStruct((4, QN, 128), BF)
    out = pl.pallas_call(
        attn_kernel,
        in_specs=[pl.BlockSpec(memory_space=pltpu.VMEM)] * 5,
        out_specs=[pl.BlockSpec(memory_space=pltpu.VMEM)] * 5,
        out_shape=[jax.ShapeDtypeStruct((QN, 128), BF)] + [slab] * 4,
        scratch_shapes=[pltpu.VMEM((4, 4, 128, QN), BF)],
        compiler_params=pltpu.CompilerParams(vmem_limit_bytes=40 * 1024 * 1024),
        cost_estimate=pl.CostEstimate(
            flops=7 * 2 * 512 * 8192 * 128, bytes_accessed=4500000, transcendentals=2 * 512 * 8192
        ),
    )(qd, *kvs)
    return out[0], out[1:]


def swap_cores(v):
    return lax.ppermute(v, "c", [(0, 1), (1, 0)])


def swap_pair(v):
    return lax.ppermute(v, "y", [(0, 1), (1, 0)])


def join(which, own, other, axis):
    return jnp.where(
        which == 0,
        jnp.concatenate([own, other], axis=axis),
        jnp.concatenate([other, own], axis=axis),
    )


def pick(which, v, axis):
    size = v.shape[axis] // 2
    lo = lax.slice_in_dim(v, 0, size, axis=axis)
    hi = lax.slice_in_dim(v, size, 2 * size, axis=axis)
    return jnp.where(which == 0, lo, hi), jnp.where(which == 0, hi, lo)


def spread(block, order):
    return lax.all_to_all(jnp.broadcast_to(block[None], (64,) + block.shape), order, 0, 0)


ROWS = ("dp", "x", "y", "z")
COLS = ("z", "dp", "x", "y")


RING = ("dp", "y")


def ring_permute(v, axis, step):
    return lax.ppermute(v, axis, [(i, (i + step) % 4) for i in range(4)])


def key_gather(v):
    level = jnp.stack([v] + [ring_permute(v, "z", i) for i in (1, 2, 3)])
    ahead = [[(k, k + j) for k in range(4 - j)] for j in (1, 2, 3)]
    return [level] + [lax.ppermute(level, "x", pairs) for pairs in ahead]


def key_sum_x(slabs):
    total = slabs[0].astype(F32)
    for j in (1, 2, 3):
        total += lax.ppermute(slabs[j], "x", [(k, k - j) for k in range(j, 4)]).astype(F32)
    return total.astype(BF)


def key_sum_z(level):
    total = level[0].astype(F32)
    for i in (1, 2, 3):
        total += ring_permute(level[i], "z", -i).astype(F32)
    return total.astype(BF)


def ring_gather(v, axis):
    me = lax.axis_index(axis)
    got = [v] + [ring_permute(v, axis, k) for k in (1, 2, 3)]
    pieces = []
    for j in range(4):
        k = (me - j) % 4
        pieces.append(jnp.where(k == 0, got[0], jnp.where(k == 1, got[1], jnp.where(k == 2, got[2], got[3]))))
    return jnp.stack(pieces)


def ring_sum(v, axis):
    me = lax.axis_index(axis)
    total = None
    for k in range(4):
        to = (me + k) % 4
        part = jnp.where(to == 0, v[0], jnp.where(to == 1, v[1], jnp.where(to == 2, v[2], v[3])))
        part = (part if k == 0 else ring_permute(part, axis, k)).astype(F32)
        total = part if total is None else total + part
    return total


def local(
    tokens,
    first_gain,
    first_shift,
    second_gain,
    second_shift,
    qkv_weight,
    out_weight,
    up_weight,
    down_weight,
    cotangent,
):
    x = lax.axis_index("x")
    y = lax.axis_index("y")
    z = lax.axis_index("z")
    c = lax.axis_index("c")

    qkv_cols = qkv_weight.reshape(6, 2, 6, 3, HS)
    q_cols = qkv_cols[:, :, :, 0].reshape(6, 2, 1, 384)
    kv_cols = qkv_cols[:, :, :, 1:].reshape(6, 2, 2, 384)
    out_cols = out_weight.reshape(6, 2, 1, 384)
    pack_one = jnp.transpose(jnp.concatenate([q_cols, kv_cols, out_cols], axis=2), (2, 1, 0, 3))
    pack_up = jnp.transpose(up_weight.reshape(6, 2, 4, 384), (2, 1, 0, 3))
    vecs = jnp.stack([first_gain, first_shift, second_gain, second_shift], axis=1)
    vecs = jnp.broadcast_to(jnp.pad(vecs, ((0, 0), (0, 124)))[None], (8, 6, 128))
    pack = jnp.concatenate([pack_one.reshape(8, 6, 384), pack_up.reshape(8, 6, 384), vecs], axis=2)
    pack = lax.all_to_all(pack, ("z", "c"), 0, 0).reshape(48, 896)
    down_keep, down_send = pick(c, down_weight, 1)
    down_rows = join(c, down_keep, swap_cores(down_send), 0)
    near = ring_gather(jnp.concatenate([pack, down_rows], axis=1), RING)
    vecs = ring_gather(near[:, :, 768:896], "x").reshape(4, 2, 2, 48, 128)
    vecs = jnp.transpose(vecs, (1, 0, 2, 3, 4)).reshape(D, 128)[:, :4].T.astype(F32)

    def by_column(v):
        return jnp.transpose(v.reshape(4, 4, 2, 2, 48, 384), (0, 2, 1, 3, 4, 5)).reshape(4, D, 384)

    one = lax.all_to_all(
        jnp.broadcast_to(near[None, :, :, :384], (16, 4, 48, 384)), ("z", "x"), 0, 0
    )
    one = by_column(one)
    two = jnp.concatenate([near[:, :, 384:768], near[:, :, 896:]], axis=1).reshape(384, 384)
    two = lax.all_gather(two, ("z", "x"), axis=0, tiled=True).reshape(4, 4, 4, 96, 384)
    up = by_column(two[:, :, :, :48])
    down = jnp.transpose(two[:, :, :, 48:].reshape(4, 4, 2, 2, 48, 384), (2, 1, 3, 0, 4, 5))
    down = down.reshape(FF, 384)

    tok = join(c, tokens, swap_cores(tokens), 0)
    cot = join(c, cotangent, swap_cores(cotangent), 0)
    cot_mine, cot_other = pick(c, cot, 1)

    out_own, out_send = pick(c, one[3], 0)
    out_got = swap_cores(out_send)

    tok_f32 = tok.astype(F32)
    first_low = layer_norm(tok_f32, vecs[0], vecs[1]).astype(BF)
    second_low = layer_norm(tok_f32, vecs[2], vecs[3]).astype(BF)

    places = ((x * 8 + y * 4 + z) * 256 + jnp.arange(256, dtype=jnp.int32)).astype(F32)
    lane = jnp.arange(128, dtype=jnp.int32)
    entry = lane % HS
    inverse = 1.0 / 10000.0 ** (2.0 * (entry % 8).astype(F32) / ROT)
    angles = places[:, None] * inverse[None, :]
    cos_v, sin_v = jnp.cos(angles), jnp.sin(angles)

    def tables(on, copies):
        cos_t = jnp.where(on, cos_v, 1.0)
        lo = jnp.where(on & (entry < 8), -sin_v, 0.0)
        hi = jnp.where(on & (entry >= 8), sin_v, 0.0)
        return tuple(jnp.tile(t, (1, copies)) for t in (cos_t, lo, hi))

    q_tab = tables(entry < ROT, 3)
    kv_tab = tables((entry < ROT) & (lane < HS), 3)

    def rotate(v, tab, sign):
        cos_t, lo, hi = tab
        return v * cos_t + sign * (jnp.roll(v, 8, axis=1) * hi + jnp.roll(v, -8, axis=1) * lo)

    query = (rotate(dot(first_low, one[0]), q_tab, 1.0) * HS ** (-0.5)).astype(BF)
    key_val = jnp.concatenate(
        [rotate(dot(first_low, one[1 + i]), kv_tab, 1.0).astype(BF) for i in range(2)], axis=1
    )
    heads_grad = (
        dot(cot_mine, out_own, ((1,), (1,))) + dot(cot_other, out_got, ((1,), (1,)))
    ).astype(BF)
    query_grad_pair = jnp.stack(
        [query.reshape(256, 6, HS), heads_grad.reshape(256, 6, HS)], axis=2
    ).reshape(256, 768)
    qd_own, qd_send = pick(y, query_grad_pair, 1)
    kv_own, kv_send = pick(y, key_val, 1)
    kv = join(y, kv_own, swap_pair(kv_send), 0)
    qd = join(y, qd_own, swap_pair(qd_send), 0)
    kv_all = [
        key_gather(kv[:, 128 * h : 128 * h + 128]) for h in range(GH)
    ]

    down_own, down_give = pick(c, down, 0)
    down_got = swap_cores(down_give)
    hidden = jnp.concatenate([dot(second_low, up[i]) for i in range(4)], axis=1)
    activated, gelu_pull = jax.vjp(exact_gelu, hidden)
    act_own = activated.astype(BF)
    act = join(c, act_own, swap_cores(act_own), 1)
    act_grad = dot(cot_mine, down_own, ((1,), (1,))) + dot(cot_other, down_got, ((1,), (1,)))
    (hidden_grad,) = gelu_pull(act_grad)
    hidden_low = hidden_grad.astype(BF)
    feed_out = dot(act, down)
    up_grad = jnp.stack(
        [
            dot(second_low, hidden_low[:, 384 * i : 384 * i + 384], ((0,), (0,))).astype(BF)
            for i in range(4)
        ]
    )
    down_grad = dot(act, cot_mine, ((0,), (0,))).astype(BF)
    second_in = sum(
        dot(hidden_low[:, 384 * i : 384 * i + 384], up[i], ((1,), (1,))) for i in range(4)
    )
    second_keep, second_send = pick(c, second_in, 0)
    second_in = second_keep + swap_cores(second_send)

    up_far = jnp.transpose(up_grad.reshape(4, 2, 4, 2, 48, 384), (0, 2, 1, 3, 4, 5))
    down_far = jnp.transpose(down_grad.reshape(2, 4, 2, 4, 48, 384), (3, 1, 0, 2, 4, 5))
    two_grad = jnp.concatenate(
        [up_far.reshape(64, 48, 384), down_far.reshape(64, 48, 384)], axis=1
    ).reshape(64 * 96, 384)
    two_near = lax.psum_scatter(two_grad, ("z", "x"), scatter_dimension=0, tiled=True)

    def head(h, tie):
        operands = (kv_all[h], qd[:, 128 * h : 128 * h + 128], tie)
        kv_h, qd_h, _ = lax.optimization_barrier(operands)
        return attention(qd_h, kv_h)

    oq_a, dkv_a = head(0, two_grad)
    level_a = key_sum_x(dkv_a)
    oq_b, dkv_b = head(1, oq_a)
    level_b = key_sum_x(dkv_b)
    oq_c, dkv_c = head(2, (oq_b, level_a))
    dkv_c, level_b = lax.optimization_barrier((dkv_c, level_b))
    level_c = key_sum_x(dkv_c)
    oq = jnp.stack([oq_a, oq_b, oq_c], axis=1).reshape(QN, GH, 2, HS)
    dkv_mine = key_sum_z(jnp.concatenate([level_a, level_b, level_c], axis=2))

    two_sum = ring_sum(two_near.reshape(4, 96, 384), RING)
    up_sum = two_sum[:48]
    down_sum = two_sum[48:]
    down_mine, down_theirs = pick(c, down_sum, 0)
    down_out = join(c, down_mine, swap_cores(down_theirs), 1)

    o_own, o_send = pick(y, oq[:, :, 1].reshape(QN, GH * HS), 0)
    heads_c = join(y, o_own, swap_pair(o_send), 1)
    heads_low = join(c, heads_c, swap_cores(heads_c), 1)
    tok_mine, _ = pick(c, tok, 1)
    half_out = (tok_mine.astype(F32) + dot(heads_low, one[3]) + feed_out).astype(BF)
    half_keep, half_send = pick(c, half_out, 0)
    layer_out = join(c, half_keep, swap_cores(half_send), 1)
    out_grad = dot(heads_low, cot_mine, ((0,), (0,))).astype(BF)

    dq_own, dq_send = pick(y, oq[:, :, 0].reshape(QN, GH * HS), 0)
    dq = join(y, dq_own, swap_pair(dq_send), 1)
    dkv_own, dkv_send = pick(y, dkv_mine, 0)
    dkv_full = join(y, dkv_own, swap_pair(dkv_send), 1)
    pre = [rotate(dq.astype(F32), q_tab, -1.0).astype(BF)] + [
        rotate(dkv_full[:, 384 * i : 384 * i + 384].astype(F32), kv_tab, -1.0).astype(BF)
        for i in range(2)
    ]
    first_in = sum(dot(pre[i], one[i], ((1,), (1,))) for i in range(3))
    first_keep, first_send = pick(c, first_in, 0)
    first_in = first_keep + swap_cores(first_send)
    one_grad = jnp.stack([dot(first_low, p, ((0,), (0,))).astype(BF) for p in pre] + [out_grad])
    one_parts = lax.all_to_all(one_grad.reshape(64, 48, 384), COLS, 0, 0)
    one_total = jnp.sum(one_parts.astype(F32), axis=0)
    rows_f32 = tokens.astype(F32)
    _, first_pull = jax.vjp(layer_norm, rows_f32, vecs[0], vecs[1])
    _, second_pull = jax.vjp(layer_norm, rows_f32, vecs[2], vecs[3])
    second_rows, gain_two_grad, shift_two_grad = second_pull(second_in)
    first_rows, gain_one_grad, shift_one_grad = first_pull(first_in)
    tokens_grad = (cotangent.astype(F32) + first_rows + second_rows).astype(BF)
    vec_grad = jnp.stack([gain_one_grad, shift_one_grad, gain_two_grad, shift_two_grad])
    vec_grad = jnp.transpose(vec_grad.reshape(4, 2, 4, 2, 48), (1, 3, 2, 0, 4)).reshape(4, 4, 4, 48)
    vec_grad = jnp.pad(vec_grad, ((0, 0), (0, 0), (0, 4), (0, 80)))
    vec_part = ring_sum(ring_sum(vec_grad, RING), "x")[:4, :48]
    vec_part = jnp.pad(vec_part.T, ((0, 0), (0, 124))).reshape(8, 6, 128)

    last = jnp.concatenate([one_total.reshape(8, 6, 384), up_sum.reshape(8, 6, 384), vec_part], axis=2)
    last = lax.all_to_all(last, ("z", "c"), 0, 0)
    one_sum = last[:, :, :384].reshape(4, 2, 6, 384)
    up_out = jnp.transpose(last[:, :, 384:768].reshape(4, 2, 6, 384), (2, 1, 0, 3)).reshape(6, FF)
    vec_out = jnp.sum(last[:, :, 768:772], axis=0).T
    out_out = one_sum[3].transpose(1, 0, 2).reshape(6, D)
    q_sum = one_sum[0].transpose(1, 0, 2).reshape(6, 2, 6, 1, HS)
    kv_sum = one_sum[1:3].transpose(2, 1, 0, 3).reshape(6, 2, 6, 2, HS)
    qkv_out = jnp.concatenate([q_sum, kv_sum], axis=3).reshape(6, 3 * D)

    return (
        layer_out,
        tokens_grad,
        vec_out[0],
        vec_out[1],
        vec_out[2],
        vec_out[3],
        qkv_out,
        out_out,
        up_out,
        down_out,
    )


def solution(mesh):
    fine = Mesh(mesh.devices.reshape(2, 4, 2, 4, 2), ALL)
    rows = P(ALL, None)
    vec = P(ALL)
    in_specs = (rows, vec, vec, vec, vec, rows, rows, rows, rows, rows)
    out_specs = (rows, rows, vec, vec, vec, vec, rows, rows, rows, rows)
    return jax.shard_map(local, mesh=fine, in_specs=in_specs, out_specs=out_specs, check_vma=False)
```

```python
import functools

import jax
import jax.numpy as jnp
from jax import lax
from jax.experimental import pallas as pl
from jax.experimental.pallas import tpu as pltpu
from jax.sharding import Mesh, PartitionSpec as P

H = 12
HS = 64
ROT = 16
D = 768
FF = 3072
EPSILON = 1e-05
BF = jnp.bfloat16
F32 = jnp.float32
CHIPS = ("dp", "x", "y", "z")
ALL = ("dp", "x", "y", "z", "c")
GH = 3
QN = 512
SLAB = 2048


def layer_norm(values, gain_vec, shift_vec):
    middle = jnp.mean(values, axis=-1, keepdims=True)
    centred = values - middle
    spread = jnp.mean(centred * centred, axis=-1, keepdims=True)
    return centred * lax.rsqrt(spread + EPSILON) * gain_vec + shift_vec


def exact_gelu(values):
    return jax.nn.gelu(values, approximate=False)


def dot(a, b, dims=((1,), (0,))):
    return lax.dot_general(a, b, (dims, ((), ())), preferred_element_type=F32)


def attn_kernel(qd_ref, *refs):
    kv_refs, oq_ref, d_refs = refs[:4], refs[4], refs[5:9]
    kt_ref, s_ref = refs[9:]
    x = lax.axis_index("x")
    z = lax.axis_index("z")
    qd = qd_ref[...]
    lane = lax.broadcasted_iota(jnp.int32, (QN, 128), 1)
    zero = jnp.zeros_like(qd)
    q0 = jnp.where(lane < HS, qd, zero)
    do0 = jnp.where(lane >= HS, qd, zero)
    q_t = q0.astype(F32).T.astype(BF)
    do_f = do0.astype(F32).T
    do_t = do_f.astype(BF)
    col = lax.broadcasted_iota(jnp.int32, (1, QN), 1)
    q_place = (col // 256) * 1024 + z * 256 + col % 256
    krow = lax.broadcasted_iota(jnp.int32, (SLAB, 1), 0)
    k_place = ((krow % 512) // 256) * 1024 + krow % 256 + ((z - krow // 512 + 4) % 4) * 256

    def fwd(_, carry, slab):
        m, l, acc = carry
        k = kv_refs[slab][...].reshape(SLAB, 128)
        k_t = k.astype(F32).T.astype(BF)
        kt_ref[slab] = k_t
        s = dot(k, q_t)
        if slab == 0:
            s = jnp.where(k_place <= q_place, s, -1e30)
        s_ref[slab] = s
        m_new = jnp.maximum(m, jnp.max(s, axis=0, keepdims=True))
        p = jnp.exp(s - m_new)
        alpha = jnp.exp(m - m_new)
        l = l * alpha + jnp.sum(p, axis=0, keepdims=True)
        acc = acc * alpha + dot(k_t, p.astype(BF))
        return m_new, l, acc

    carry = (
        jnp.full((1, QN), -1e30, F32),
        jnp.zeros((1, QN), F32),
        jnp.zeros((128, QN), F32),
    )
    for slab in range(4):
        count = jnp.where(x >= slab, 1, 0)
        carry = lax.fori_loop(0, count, functools.partial(fwd, slab=slab), carry)
    m, l, acc = carry
    lse = m + jnp.log(l)
    o_low = (acc / l).astype(BF).astype(F32)
    delta = jnp.sum(do_f * o_low, axis=0, keepdims=True)

    def bwd(_, dq, slab):
        k = kv_refs[slab][...].reshape(SLAB, 128)
        p = jnp.exp(s_ref[slab] - lse)
        dp = dot(k, do_t)
        ds = (p * (dp - delta)).astype(BF)
        d_kv = dot(ds, q0) + dot(p.astype(BF), do0)
        d_refs[slab][...] = d_kv.astype(BF).reshape(4, QN, 128)
        return dq + dot(kt_ref[slab], ds)

    dq = jnp.zeros((128, QN), F32)
    for slab in range(4):
        count = jnp.where(x >= slab, 1, 0)
        dq = lax.fori_loop(0, count, functools.partial(bwd, slab=slab), dq)
        if slab > 0:

            @pl.when(x < slab)
            def _():
                d_refs[slab][...] = jnp.zeros((4, QN, 128), BF)

    row = lax.broadcasted_iota(jnp.int32, (128, QN), 0)
    oq_ref[...] = jnp.where(row < HS, dq * HS ** (-0.5), o_low).T.astype(BF)


def attention(qd, kvs):
    slab = jax.ShapeDtypeStruct((4, QN, 128), BF)
    out = pl.pallas_call(
        attn_kernel,
        in_specs=[pl.BlockSpec(memory_space=pltpu.VMEM)] * 5,
        out_specs=[pl.BlockSpec(memory_space=pltpu.VMEM)] * 5,
        out_shape=[jax.ShapeDtypeStruct((QN, 128), BF)] + [slab] * 4,
        scratch_shapes=[pltpu.VMEM((4, 128, SLAB), BF), pltpu.VMEM((4, SLAB, QN), F32)],
        compiler_params=pltpu.CompilerParams(vmem_limit_bytes=48 * 1024 * 1024),
        cost_estimate=pl.CostEstimate(
            flops=7 * 2 * 512 * 8192 * 128, bytes_accessed=4500000, transcendentals=2 * 512 * 8192
        ),
    )(qd, *kvs)
    return out[0], out[1:]


def swap_cores(v):
    return lax.ppermute(v, "c", [(0, 1), (1, 0)])


def swap_pair(v):
    return lax.ppermute(v, "y", [(0, 1), (1, 0)])


def join(which, own, other, axis):
    return jnp.where(
        which == 0,
        jnp.concatenate([own, other], axis=axis),
        jnp.concatenate([other, own], axis=axis),
    )


def pick(which, v, axis):
    size = v.shape[axis] // 2
    lo = lax.slice_in_dim(v, 0, size, axis=axis)
    hi = lax.slice_in_dim(v, size, 2 * size, axis=axis)
    return jnp.where(which == 0, lo, hi), jnp.where(which == 0, hi, lo)


def spread(block, order):
    return lax.all_to_all(jnp.broadcast_to(block[None], (64,) + block.shape), order, 0, 0)


ROWS = ("dp", "x", "y", "z")
COLS = ("z", "dp", "x", "y")


RING = ("dp", "y")


def ring_permute(v, axis, step):
    return lax.ppermute(v, axis, [(i, (i + step) % 4) for i in range(4)])


def key_gather(v):
    level = jnp.stack([v] + [ring_permute(v, "z", i) for i in (1, 2, 3)])
    ahead = [[(k, k + j) for k in range(4 - j)] for j in (1, 2, 3)]
    return [level] + [lax.ppermute(level, "x", pairs) for pairs in ahead]


def key_sum_x(slabs):
    total = slabs[0].astype(F32)
    for j in (1, 2, 3):
        total += lax.ppermute(slabs[j], "x", [(k, k - j) for k in range(j, 4)]).astype(F32)
    return total.astype(BF)


def key_sum_z(level):
    total = level[0].astype(F32)
    for i in (1, 2, 3):
        total += ring_permute(level[i], "z", -i).astype(F32)
    return total.astype(BF)


def ring_gather(v, axis):
    me = lax.axis_index(axis)
    got = [v] + [ring_permute(v, axis, k) for k in (1, 2, 3)]
    pieces = []
    for j in range(4):
        k = (me - j) % 4
        pieces.append(jnp.where(k == 0, got[0], jnp.where(k == 1, got[1], jnp.where(k == 2, got[2], got[3]))))
    return jnp.stack(pieces)


def ring_sum(v, axis):
    me = lax.axis_index(axis)
    total = None
    for k in range(4):
        to = (me + k) % 4
        part = jnp.where(to == 0, v[0], jnp.where(to == 1, v[1], jnp.where(to == 2, v[2], v[3])))
        part = (part if k == 0 else ring_permute(part, axis, k)).astype(F32)
        total = part if total is None else total + part
    return total


def local(
    tokens,
    first_gain,
    first_shift,
    second_gain,
    second_shift,
    qkv_weight,
    out_weight,
    up_weight,
    down_weight,
    cotangent,
):
    x = lax.axis_index("x")
    y = lax.axis_index("y")
    z = lax.axis_index("z")
    c = lax.axis_index("c")

    qkv_cols = qkv_weight.reshape(6, 2, 6, 3, HS)
    q_cols = qkv_cols[:, :, :, 0].reshape(6, 2, 1, 384)
    kv_cols = qkv_cols[:, :, :, 1:].reshape(6, 2, 2, 384)
    out_cols = out_weight.reshape(6, 2, 1, 384)
    pack_one = jnp.transpose(jnp.concatenate([q_cols, kv_cols, out_cols], axis=2), (2, 1, 0, 3))
    pack_up = jnp.transpose(up_weight.reshape(6, 2, 4, 384), (2, 1, 0, 3))
    vecs = jnp.stack([first_gain, first_shift, second_gain, second_shift], axis=1)
    vecs = jnp.broadcast_to(jnp.pad(vecs, ((0, 0), (0, 124)))[None], (8, 6, 128))
    pack = jnp.concatenate([pack_one.reshape(8, 6, 384), pack_up.reshape(8, 6, 384), vecs], axis=2)
    pack = lax.all_to_all(pack, ("z", "c"), 0, 0).reshape(48, 896)
    down_keep, down_send = pick(c, down_weight, 1)
    down_rows = join(c, down_keep, swap_cores(down_send), 0)
    near = ring_gather(jnp.concatenate([pack, down_rows], axis=1), RING)
    vecs = ring_gather(near[:, :, 768:896], "x").reshape(4, 2, 2, 48, 128)
    vecs = jnp.transpose(vecs, (1, 0, 2, 3, 4)).reshape(D, 128)[:, :4].T.astype(F32)

    def by_column(v):
        return jnp.transpose(v.reshape(4, 4, 2, 2, 48, 384), (0, 2, 1, 3, 4, 5)).reshape(4, D, 384)

    one = lax.all_to_all(
        jnp.broadcast_to(near[None, :, :, :384], (16, 4, 48, 384)), ("z", "x"), 0, 0
    )
    one = by_column(one)
    two = jnp.concatenate([near[:, :, 384:768], near[:, :, 896:]], axis=1).reshape(384, 384)
    two = lax.all_gather(two, ("z", "x"), axis=0, tiled=True).reshape(4, 4, 4, 96, 384)
    up = by_column(two[:, :, :, :48])
    down = jnp.transpose(two[:, :, :, 48:].reshape(4, 4, 2, 2, 48, 384), (2, 1, 3, 0, 4, 5))
    down = down.reshape(FF, 384)

    tok = join(c, tokens, swap_cores(tokens), 0)
    cot = join(c, cotangent, swap_cores(cotangent), 0)
    cot_mine, cot_other = pick(c, cot, 1)

    out_own, out_send = pick(c, one[3], 0)
    out_got = swap_cores(out_send)

    tok_f32 = tok.astype(F32)
    first_low = layer_norm(tok_f32, vecs[0], vecs[1]).astype(BF)
    second_low = layer_norm(tok_f32, vecs[2], vecs[3]).astype(BF)

    places = ((x * 8 + y * 4 + z) * 256 + jnp.arange(256, dtype=jnp.int32)).astype(F32)
    lane = jnp.arange(128, dtype=jnp.int32)
    entry = lane % HS
    inverse = 1.0 / 10000.0 ** (2.0 * (entry % 8).astype(F32) / ROT)
    angles = places[:, None] * inverse[None, :]
    cos_v, sin_v = jnp.cos(angles), jnp.sin(angles)

    def tables(on, copies):
        cos_t = jnp.where(on, cos_v, 1.0)
        lo = jnp.where(on & (entry < 8), -sin_v, 0.0)
        hi = jnp.where(on & (entry >= 8), sin_v, 0.0)
        return tuple(jnp.tile(t, (1, copies)) for t in (cos_t, lo, hi))

    q_tab = tables(entry < ROT, 3)
    kv_tab = tables((entry < ROT) & (lane < HS), 3)

    def rotate(v, tab, sign):
        cos_t, lo, hi = tab
        return v * cos_t + sign * (jnp.roll(v, 8, axis=1) * hi + jnp.roll(v, -8, axis=1) * lo)

    query = (rotate(dot(first_low, one[0]), q_tab, 1.0) * HS ** (-0.5)).astype(BF)
    key_val = jnp.concatenate(
        [rotate(dot(first_low, one[1 + i]), kv_tab, 1.0).astype(BF) for i in range(2)], axis=1
    )
    heads_grad = (
        dot(cot_mine, out_own, ((1,), (1,))) + dot(cot_other, out_got, ((1,), (1,)))
    ).astype(BF)
    query_grad_pair = jnp.stack(
        [query.reshape(256, 6, HS), heads_grad.reshape(256, 6, HS)], axis=2
    ).reshape(256, 768)
    qd_own, qd_send = pick(y, query_grad_pair, 1)
    kv_own, kv_send = pick(y, key_val, 1)
    kv = join(y, kv_own, swap_pair(kv_send), 0)
    qd = join(y, qd_own, swap_pair(qd_send), 0)
    kv_all = [
        key_gather(kv[:, 128 * h : 128 * h + 128]) for h in range(GH)
    ]

    down_own, down_give = pick(c, down, 0)
    down_got = swap_cores(down_give)
    hidden = jnp.concatenate([dot(second_low, up[i]) for i in range(4)], axis=1)
    activated, gelu_pull = jax.vjp(exact_gelu, hidden)
    act_own = activated.astype(BF)
    act = join(c, act_own, swap_cores(act_own), 1)
    act_grad = dot(cot_mine, down_own, ((1,), (1,))) + dot(cot_other, down_got, ((1,), (1,)))
    (hidden_grad,) = gelu_pull(act_grad)
    hidden_low = hidden_grad.astype(BF)
    feed_out = dot(act, down)
    up_grad = jnp.stack(
        [
            dot(second_low, hidden_low[:, 384 * i : 384 * i + 384], ((0,), (0,))).astype(BF)
            for i in range(4)
        ]
    )
    down_grad = dot(act, cot_mine, ((0,), (0,))).astype(BF)
    second_in = sum(
        dot(hidden_low[:, 384 * i : 384 * i + 384], up[i], ((1,), (1,))) for i in range(4)
    )
    tok_norm = layer_norm(tok_f32, 1.0, 0.0)
    gain_two_grad, shift_two_grad = jnp.sum(second_in * tok_norm, axis=0), jnp.sum(second_in, axis=0)
    second_keep, second_send = pick(c, second_in, 0)
    second_in = second_keep + swap_cores(second_send)

    up_far = jnp.transpose(up_grad.reshape(4, 2, 4, 2, 48, 384), (0, 2, 1, 3, 4, 5))
    down_far = jnp.transpose(down_grad.reshape(2, 4, 2, 4, 48, 384), (3, 1, 0, 2, 4, 5))
    two_grad = jnp.concatenate(
        [up_far.reshape(64, 48, 384), down_far.reshape(64, 48, 384)], axis=1
    ).reshape(64 * 96, 384)
    two_near = lax.psum_scatter(two_grad, ("z", "x"), scatter_dimension=0, tiled=True)

    def head(h, tie):
        operands = (kv_all[h], qd[:, 128 * h : 128 * h + 128], tie)
        kv_h, qd_h, _ = lax.optimization_barrier(operands)
        return attention(qd_h, kv_h)

    oq_a, dkv_a = head(0, two_grad)
    level_a = key_sum_x(dkv_a)
    oq_b, dkv_b = head(1, oq_a)
    level_b = key_sum_x(dkv_b)
    oq_c, dkv_c = head(2, (oq_b, level_a))
    dkv_c, level_b = lax.optimization_barrier((dkv_c, level_b))
    level_c = key_sum_x(dkv_c)
    oq = jnp.stack([oq_a, oq_b, oq_c], axis=1).reshape(QN, GH, 2, HS)
    dkv_mine = key_sum_z(jnp.concatenate([level_a, level_b, level_c], axis=2))

    two_sum = ring_sum(two_near.reshape(4, 96, 384), RING)
    up_sum = two_sum[:48]
    down_sum = two_sum[48:]
    down_mine, down_theirs = pick(c, down_sum, 0)
    down_out = join(c, down_mine, swap_cores(down_theirs), 1)

    o_own, o_send = pick(y, oq[:, :, 1].reshape(QN, GH * HS), 0)
    heads_c = join(y, o_own, swap_pair(o_send), 1)
    heads_low = join(c, heads_c, swap_cores(heads_c), 1)
    tok_mine, _ = pick(c, tok, 1)
    half_out = (tok_mine.astype(F32) + dot(heads_low, one[3]) + feed_out).astype(BF)
    half_keep, half_send = pick(c, half_out, 0)
    layer_out = join(c, half_keep, swap_cores(half_send), 1)
    out_grad = dot(heads_low, cot_mine, ((0,), (0,))).astype(BF)

    dq_own, dq_send = pick(y, oq[:, :, 0].reshape(QN, GH * HS), 0)
    dq = join(y, dq_own, swap_pair(dq_send), 1)
    dkv_own, dkv_send = pick(y, dkv_mine, 0)
    dkv_full = join(y, dkv_own, swap_pair(dkv_send), 1)
    pre = [rotate(dq.astype(F32), q_tab, -1.0).astype(BF)] + [
        rotate(dkv_full[:, 384 * i : 384 * i + 384].astype(F32), kv_tab, -1.0).astype(BF)
        for i in range(2)
    ]
    first_in = sum(dot(pre[i], one[i], ((1,), (1,))) for i in range(3))
    gain_one_grad, shift_one_grad = jnp.sum(first_in * tok_norm, axis=0), jnp.sum(first_in, axis=0)
    first_keep, first_send = pick(c, first_in, 0)
    first_in = first_keep + swap_cores(first_send)
    one_grad = jnp.stack([dot(first_low, p, ((0,), (0,))).astype(BF) for p in pre] + [out_grad])
    one_parts = lax.all_to_all(one_grad.reshape(64, 48, 384), COLS, 0, 0)
    one_total = jnp.sum(one_parts.astype(F32), axis=0)
    rows_f32 = tokens.astype(F32)
    _, first_pull = jax.vjp(layer_norm, rows_f32, vecs[0], vecs[1])
    _, second_pull = jax.vjp(layer_norm, rows_f32, vecs[2], vecs[3])
    second_rows = second_pull(second_in)[0]
    first_rows = first_pull(first_in)[0]
    tokens_grad = (cotangent.astype(F32) + first_rows + second_rows).astype(BF)
    vec_grad = jnp.stack([gain_one_grad, shift_one_grad, gain_two_grad, shift_two_grad])
    vec_grad = jnp.transpose(vec_grad.reshape(4, 2, 4, 2, 48), (1, 3, 2, 0, 4)).reshape(4, 4, 4, 48)
    vec_grad = jnp.pad(vec_grad, ((0, 0), (0, 0), (0, 4), (0, 80)))
    vec_part = ring_sum(ring_sum(vec_grad, RING), "x")[:4, :48]
    vec_part = jnp.pad(vec_part.T, ((0, 0), (0, 124))).reshape(8, 6, 128)

    last = jnp.concatenate([one_total.reshape(8, 6, 384), up_sum.reshape(8, 6, 384), vec_part], axis=2)
    last = lax.all_to_all(last, ("z", "c"), 0, 0)
    one_sum = last[:, :, :384].reshape(4, 2, 6, 384)
    up_out = jnp.transpose(last[:, :, 384:768].reshape(4, 2, 6, 384), (2, 1, 0, 3)).reshape(6, FF)
    vec_out = jnp.sum(last[:, :, 768:772], axis=0).T
    out_out = one_sum[3].transpose(1, 0, 2).reshape(6, D)
    q_sum = one_sum[0].transpose(1, 0, 2).reshape(6, 2, 6, 1, HS)
    kv_sum = one_sum[1:3].transpose(2, 1, 0, 3).reshape(6, 2, 6, 2, HS)
    qkv_out = jnp.concatenate([q_sum, kv_sum], axis=3).reshape(6, 3 * D)

    return (
        layer_out,
        tokens_grad,
        vec_out[0],
        vec_out[1],
        vec_out[2],
        vec_out[3],
        qkv_out,
        out_out,
        up_out,
        down_out,
    )


def solution(mesh):
    fine = Mesh(mesh.devices.reshape(2, 4, 2, 4, 2), ALL)
    rows = P(ALL, None)
    vec = P(ALL)
    in_specs = (rows, vec, vec, vec, vec, rows, rows, rows, rows, rows)
    out_specs = (rows, rows, vec, vec, vec, vec, rows, rows, rows, rows)
    return jax.shard_map(local, mesh=fine, in_specs=in_specs, out_specs=out_specs, check_vma=False)
```

```python
import functools

import jax
import jax.numpy as jnp
from jax import lax
from jax.experimental import pallas as pl
from jax.experimental.pallas import tpu as pltpu
from jax.sharding import Mesh, PartitionSpec as P

H = 12
HS = 64
ROT = 16
D = 768
FF = 3072
EPSILON = 1e-05
BF = jnp.bfloat16
F32 = jnp.float32
CHIPS = ("dp", "x", "y", "z")
ALL = ("dp", "x", "y", "z", "c")
GH = 3
QN = 512
SLAB = 2048


def layer_norm(values, gain_vec, shift_vec):
    middle = jnp.mean(values, axis=-1, keepdims=True)
    centred = values - middle
    spread = jnp.mean(centred * centred, axis=-1, keepdims=True)
    return centred * lax.rsqrt(spread + EPSILON) * gain_vec + shift_vec


def exact_gelu(values):
    return jax.nn.gelu(values, approximate=False)


def dot(a, b, dims=((1,), (0,))):
    return lax.dot_general(a, b, (dims, ((), ())), preferred_element_type=F32)


def attn_kernel(qd_ref, *refs):
    kv_refs, oq_ref, d_refs = refs[:4], refs[4], refs[5:9]
    kt_ref, p_ref, m_ref = refs[9:]
    x = lax.axis_index("x")
    z = lax.axis_index("z")
    qd = qd_ref[...]
    lane = lax.broadcasted_iota(jnp.int32, (QN, 128), 1)
    zero = jnp.zeros_like(qd)
    q0 = jnp.where(lane < HS, qd, zero)
    do0 = jnp.where(lane >= HS, qd, zero)
    q_t = q0.astype(F32).T.astype(BF)
    do_f = do0.astype(F32).T
    do_t = do_f.astype(BF)
    col = lax.broadcasted_iota(jnp.int32, (1, QN), 1)
    q_place = (col // 256) * 1024 + z * 256 + col % 256
    krow = lax.broadcasted_iota(jnp.int32, (SLAB, 1), 0)
    k_place = ((krow % 512) // 256) * 1024 + krow % 256 + ((z - krow // 512 + 4) % 4) * 256

    def fwd(_, carry, slab):
        m, l, acc = carry
        k = kv_refs[slab][...].reshape(SLAB, 128)
        k_t = k.astype(F32).T.astype(BF)
        kt_ref[slab] = k_t
        s = dot(k, q_t)
        if slab == 0:
            s = jnp.where(k_place <= q_place, s, -1e30)
        m_new = jnp.maximum(m, jnp.max(s, axis=0, keepdims=True))
        p = jnp.exp(s - m_new)
        p_ref[slab] = p
        m_ref[slab] = m_new
        alpha = jnp.exp(m - m_new)
        l = l * alpha + jnp.sum(p, axis=0, keepdims=True)
        acc = acc * alpha + dot(k_t, p.astype(BF))
        return m_new, l, acc

    carry = (
        jnp.full((1, QN), -1e30, F32),
        jnp.zeros((1, QN), F32),
        jnp.zeros((128, QN), F32),
    )
    for slab in range(4):
        count = jnp.where(x >= slab, 1, 0)
        carry = lax.fori_loop(0, count, functools.partial(fwd, slab=slab), carry)
    m, l, acc = carry
    lse = m + jnp.log(l)
    o_low = (acc / l).astype(BF).astype(F32)
    delta = jnp.sum(do_f * o_low, axis=0, keepdims=True)

    def bwd(_, dq, slab):
        k = kv_refs[slab][...].reshape(SLAB, 128)
        p = p_ref[slab] * jnp.exp(m_ref[slab] - lse)
        dp = dot(k, do_t)
        ds = (p * (dp - delta)).astype(BF)
        d_kv = dot(ds, q0) + dot(p.astype(BF), do0)
        d_refs[slab][...] = d_kv.astype(BF).reshape(4, QN, 128)
        return dq + dot(kt_ref[slab], ds)

    dq = jnp.zeros((128, QN), F32)
    for slab in range(4):
        count = jnp.where(x >= slab, 1, 0)
        dq = lax.fori_loop(0, count, functools.partial(bwd, slab=slab), dq)
        if slab > 0:

            @pl.when(x < slab)
            def _():
                d_refs[slab][...] = jnp.zeros((4, QN, 128), BF)

    row = lax.broadcasted_iota(jnp.int32, (128, QN), 0)
    oq_ref[...] = jnp.where(row < HS, dq * HS ** (-0.5), o_low).T.astype(BF)


def attention(qd, kvs):
    slab = jax.ShapeDtypeStruct((4, QN, 128), BF)
    out = pl.pallas_call(
        attn_kernel,
        in_specs=[pl.BlockSpec(memory_space=pltpu.VMEM)] * 5,
        out_specs=[pl.BlockSpec(memory_space=pltpu.VMEM)] * 5,
        out_shape=[jax.ShapeDtypeStruct((QN, 128), BF)] + [slab] * 4,
        scratch_shapes=[pltpu.VMEM((4, 128, SLAB), BF), pltpu.VMEM((4, SLAB, QN), F32), pltpu.VMEM((4, 1, QN), F32)],
        compiler_params=pltpu.CompilerParams(vmem_limit_bytes=48 * 1024 * 1024),
        cost_estimate=pl.CostEstimate(
            flops=7 * 2 * 512 * 8192 * 128, bytes_accessed=4500000, transcendentals=2 * 512 * 8192
        ),
    )(qd, *kvs)
    return out[0], out[1:]


def swap_cores(v):
    return lax.ppermute(v, "c", [(0, 1), (1, 0)])


def swap_pair(v):
    return lax.ppermute(v, "y", [(0, 1), (1, 0)])


def join(which, own, other, axis):
    return jnp.where(
        which == 0,
        jnp.concatenate([own, other], axis=axis),
        jnp.concatenate([other, own], axis=axis),
    )


def pick(which, v, axis):
    size = v.shape[axis] // 2
    lo = lax.slice_in_dim(v, 0, size, axis=axis)
    hi = lax.slice_in_dim(v, size, 2 * size, axis=axis)
    return jnp.where(which == 0, lo, hi), jnp.where(which == 0, hi, lo)


def spread(block, order):
    return lax.all_to_all(jnp.broadcast_to(block[None], (64,) + block.shape), order, 0, 0)


ROWS = ("dp", "x", "y", "z")
COLS = ("z", "dp", "x", "y")


RING = ("dp", "y")


def ring_permute(v, axis, step):
    return lax.ppermute(v, axis, [(i, (i + step) % 4) for i in range(4)])


def key_gather(v):
    level = jnp.stack([v] + [ring_permute(v, "z", i) for i in (1, 2, 3)])
    ahead = [[(k, k + j) for k in range(4 - j)] for j in (1, 2, 3)]
    return [level] + [lax.ppermute(level, "x", pairs) for pairs in ahead]


def key_sum_x(slabs):
    total = slabs[0].astype(F32)
    for j in (1, 2, 3):
        total += lax.ppermute(slabs[j], "x", [(k, k - j) for k in range(j, 4)]).astype(F32)
    return total.astype(BF)


def key_sum_z(level):
    total = level[0].astype(F32)
    for i in (1, 2, 3):
        total += ring_permute(level[i], "z", -i).astype(F32)
    return total.astype(BF)


def ring_gather(v, axis):
    me = lax.axis_index(axis)
    got = [v] + [ring_permute(v, axis, k) for k in (1, 2, 3)]
    pieces = []
    for j in range(4):
        k = (me - j) % 4
        pieces.append(jnp.where(k == 0, got[0], jnp.where(k == 1, got[1], jnp.where(k == 2, got[2], got[3]))))
    return jnp.stack(pieces)


def ring_sum(v, axis):
    me = lax.axis_index(axis)
    total = None
    for k in range(4):
        to = (me + k) % 4
        part = jnp.where(to == 0, v[0], jnp.where(to == 1, v[1], jnp.where(to == 2, v[2], v[3])))
        part = (part if k == 0 else ring_permute(part, axis, k)).astype(F32)
        total = part if total is None else total + part
    return total


def local(
    tokens,
    first_gain,
    first_shift,
    second_gain,
    second_shift,
    qkv_weight,
    out_weight,
    up_weight,
    down_weight,
    cotangent,
):
    x = lax.axis_index("x")
    y = lax.axis_index("y")
    z = lax.axis_index("z")
    c = lax.axis_index("c")

    qkv_cols = qkv_weight.reshape(6, 2, 6, 3, HS)
    q_cols = qkv_cols[:, :, :, 0].reshape(6, 2, 1, 384)
    kv_cols = qkv_cols[:, :, :, 1:].reshape(6, 2, 2, 384)
    out_cols = out_weight.reshape(6, 2, 1, 384)
    pack_one = jnp.transpose(jnp.concatenate([q_cols, kv_cols, out_cols], axis=2), (2, 1, 0, 3))
    pack_up = jnp.transpose(up_weight.reshape(6, 2, 4, 384), (2, 1, 0, 3))
    vecs = jnp.stack([first_gain, first_shift, second_gain, second_shift], axis=1)
    vecs = jnp.broadcast_to(jnp.pad(vecs, ((0, 0), (0, 124)))[None], (8, 6, 128))
    pack = jnp.concatenate([pack_one.reshape(8, 6, 384), pack_up.reshape(8, 6, 384), vecs], axis=2)
    pack = lax.all_to_all(pack, ("z", "c"), 0, 0).reshape(48, 896)
    down_keep, down_send = pick(c, down_weight, 1)
    down_rows = join(c, down_keep, swap_cores(down_send), 0)
    near = ring_gather(jnp.concatenate([pack, down_rows], axis=1), RING)
    vecs = ring_gather(near[:, :, 768:896], "x").reshape(4, 2, 2, 48, 128)
    vecs = jnp.transpose(vecs, (1, 0, 2, 3, 4)).reshape(D, 128)[:, :4].T.astype(F32)

    def by_column(v):
        return jnp.transpose(v.reshape(4, 4, 2, 2, 48, 384), (0, 2, 1, 3, 4, 5)).reshape(4, D, 384)

    one = lax.all_to_all(
        jnp.broadcast_to(near[None, :, :, :384], (16, 4, 48, 384)), ("z", "x"), 0, 0
    )
    one = by_column(one)
    two = jnp.concatenate([near[:, :, 384:768], near[:, :, 896:]], axis=1).reshape(384, 384)
    two = lax.all_gather(two, ("z", "x"), axis=0, tiled=True).reshape(4, 4, 4, 96, 384)
    up = by_column(two[:, :, :, :48])
    down = jnp.transpose(two[:, :, :, 48:].reshape(4, 4, 2, 2, 48, 384), (2, 1, 3, 0, 4, 5))
    down = down.reshape(FF, 384)

    tok = join(c, tokens, swap_cores(tokens), 0)
    cot = join(c, cotangent, swap_cores(cotangent), 0)
    cot_mine, cot_other = pick(c, cot, 1)

    out_own, out_send = pick(c, one[3], 0)
    out_got = swap_cores(out_send)

    tok_f32 = tok.astype(F32)
    first_low = layer_norm(tok_f32, vecs[0], vecs[1]).astype(BF)
    second_low = layer_norm(tok_f32, vecs[2], vecs[3]).astype(BF)

    places = ((x * 8 + y * 4 + z) * 256 + jnp.arange(256, dtype=jnp.int32)).astype(F32)
    lane = jnp.arange(128, dtype=jnp.int32)
    entry = lane % HS
    inverse = 1.0 / 10000.0 ** (2.0 * (entry % 8).astype(F32) / ROT)
    angles = places[:, None] * inverse[None, :]
    cos_v, sin_v = jnp.cos(angles), jnp.sin(angles)

    def tables(on, copies):
        cos_t = jnp.where(on, cos_v, 1.0)
        lo = jnp.where(on & (entry < 8), -sin_v, 0.0)
        hi = jnp.where(on & (entry >= 8), sin_v, 0.0)
        return tuple(jnp.tile(t, (1, copies)) for t in (cos_t, lo, hi))

    q_tab = tables(entry < ROT, 3)
    kv_tab = tables((entry < ROT) & (lane < HS), 3)

    def rotate(v, tab, sign):
        cos_t, lo, hi = tab
        return v * cos_t + sign * (jnp.roll(v, 8, axis=1) * hi + jnp.roll(v, -8, axis=1) * lo)

    query = (rotate(dot(first_low, one[0]), q_tab, 1.0) * HS ** (-0.5)).astype(BF)
    key_val = jnp.concatenate(
        [rotate(dot(first_low, one[1 + i]), kv_tab, 1.0).astype(BF) for i in range(2)], axis=1
    )
    heads_grad = (
        dot(cot_mine, out_own, ((1,), (1,))) + dot(cot_other, out_got, ((1,), (1,)))
    ).astype(BF)
    query_grad_pair = jnp.stack(
        [query.reshape(256, 6, HS), heads_grad.reshape(256, 6, HS)], axis=2
    ).reshape(256, 768)
    qd_own, qd_send = pick(y, query_grad_pair, 1)
    kv_own, kv_send = pick(y, key_val, 1)
    kv = join(y, kv_own, swap_pair(kv_send), 0)
    qd = join(y, qd_own, swap_pair(qd_send), 0)
    kv_all = [
        key_gather(kv[:, 128 * h : 128 * h + 128]) for h in range(GH)
    ]

    down_own, down_give = pick(c, down, 0)
    down_got = swap_cores(down_give)
    hidden = jnp.concatenate([dot(second_low, up[i]) for i in range(4)], axis=1)
    activated, gelu_pull = jax.vjp(exact_gelu, hidden)
    act_own = activated.astype(BF)
    act = join(c, act_own, swap_cores(act_own), 1)
    act_grad = dot(cot_mine, down_own, ((1,), (1,))) + dot(cot_other, down_got, ((1,), (1,)))
    (hidden_grad,) = gelu_pull(act_grad)
    hidden_low = hidden_grad.astype(BF)
    feed_out = dot(act, down)
    up_grad = jnp.stack(
        [
            dot(second_low, hidden_low[:, 384 * i : 384 * i + 384], ((0,), (0,))).astype(BF)
            for i in range(4)
        ]
    )
    down_grad = dot(act, cot_mine, ((0,), (0,))).astype(BF)
    second_in = sum(
        dot(hidden_low[:, 384 * i : 384 * i + 384], up[i], ((1,), (1,))) for i in range(4)
    )
    tok_norm = layer_norm(tok_f32, 1.0, 0.0)
    gain_two_grad, shift_two_grad = jnp.sum(second_in * tok_norm, axis=0), jnp.sum(second_in, axis=0)
    second_keep, second_send = pick(c, second_in, 0)
    second_in = second_keep + swap_cores(second_send)

    up_far = jnp.transpose(up_grad.reshape(4, 2, 4, 2, 48, 384), (0, 2, 1, 3, 4, 5))
    down_far = jnp.transpose(down_grad.reshape(2, 4, 2, 4, 48, 384), (3, 1, 0, 2, 4, 5))
    two_grad = jnp.concatenate(
        [up_far.reshape(64, 48, 384), down_far.reshape(64, 48, 384)], axis=1
    ).reshape(64 * 96, 384)
    two_near = lax.psum_scatter(two_grad, ("z", "x"), scatter_dimension=0, tiled=True)

    def head(h, tie):
        operands = (kv_all[h], qd[:, 128 * h : 128 * h + 128], tie)
        kv_h, qd_h, _ = lax.optimization_barrier(operands)
        return attention(qd_h, kv_h)

    oq_a, dkv_a = head(0, two_grad)
    level_a = key_sum_x(dkv_a)
    oq_b, dkv_b = head(1, oq_a)
    level_b = key_sum_x(dkv_b)
    oq_c, dkv_c = head(2, (oq_b, level_a))
    dkv_c, level_b = lax.optimization_barrier((dkv_c, level_b))
    level_c = key_sum_x(dkv_c)
    oq = jnp.stack([oq_a, oq_b, oq_c], axis=1).reshape(QN, GH, 2, HS)
    dkv_mine = key_sum_z(jnp.concatenate([level_a, level_b, level_c], axis=2))

    two_sum = ring_sum(two_near.reshape(4, 96, 384), RING)
    up_sum = two_sum[:48]
    down_sum = two_sum[48:]
    down_mine, down_theirs = pick(c, down_sum, 0)
    down_out = join(c, down_mine, swap_cores(down_theirs), 1)

    o_own, o_send = pick(y, oq[:, :, 1].reshape(QN, GH * HS), 0)
    heads_c = join(y, o_own, swap_pair(o_send), 1)
    heads_low = join(c, heads_c, swap_cores(heads_c), 1)
    tok_mine, _ = pick(c, tok, 1)
    half_out = (tok_mine.astype(F32) + dot(heads_low, one[3]) + feed_out).astype(BF)
    half_keep, half_send = pick(c, half_out, 0)
    layer_out = join(c, half_keep, swap_cores(half_send), 1)
    out_grad = dot(heads_low, cot_mine, ((0,), (0,))).astype(BF)

    dq_own, dq_send = pick(y, oq[:, :, 0].reshape(QN, GH * HS), 0)
    dq = join(y, dq_own, swap_pair(dq_send), 1)
    dkv_own, dkv_send = pick(y, dkv_mine, 0)
    dkv_full = join(y, dkv_own, swap_pair(dkv_send), 1)
    pre = [rotate(dq.astype(F32), q_tab, -1.0).astype(BF)] + [
        rotate(dkv_full[:, 384 * i : 384 * i + 384].astype(F32), kv_tab, -1.0).astype(BF)
        for i in range(2)
    ]
    first_in = sum(dot(pre[i], one[i], ((1,), (1,))) for i in range(3))
    gain_one_grad, shift_one_grad = jnp.sum(first_in * tok_norm, axis=0), jnp.sum(first_in, axis=0)
    first_keep, first_send = pick(c, first_in, 0)
    first_in = first_keep + swap_cores(first_send)
    one_grad = jnp.stack([dot(first_low, p, ((0,), (0,))).astype(BF) for p in pre] + [out_grad])
    one_parts = lax.all_to_all(one_grad.reshape(64, 48, 384), COLS, 0, 0)
    one_total = jnp.sum(one_parts.astype(F32), axis=0)
    rows_f32 = tokens.astype(F32)
    _, first_pull = jax.vjp(layer_norm, rows_f32, vecs[0], vecs[1])
    _, second_pull = jax.vjp(layer_norm, rows_f32, vecs[2], vecs[3])
    second_rows = second_pull(second_in)[0]
    first_rows = first_pull(first_in)[0]
    tokens_grad = (cotangent.astype(F32) + first_rows + second_rows).astype(BF)
    vec_grad = jnp.stack([gain_one_grad, shift_one_grad, gain_two_grad, shift_two_grad])
    vec_grad = jnp.transpose(vec_grad.reshape(4, 2, 4, 2, 48), (1, 3, 2, 0, 4)).reshape(4, 4, 4, 48)
    vec_grad = jnp.pad(vec_grad, ((0, 0), (0, 0), (0, 4), (0, 80)))
    vec_part = ring_sum(ring_sum(vec_grad, RING), "x")[:4, :48]
    vec_part = jnp.pad(vec_part.T, ((0, 0), (0, 124))).reshape(8, 6, 128)

    last = jnp.concatenate([one_total.reshape(8, 6, 384), up_sum.reshape(8, 6, 384), vec_part], axis=2)
    last = lax.all_to_all(last, ("z", "c"), 0, 0)
    one_sum = last[:, :, :384].reshape(4, 2, 6, 384)
    up_out = jnp.transpose(last[:, :, 384:768].reshape(4, 2, 6, 384), (2, 1, 0, 3)).reshape(6, FF)
    vec_out = jnp.sum(last[:, :, 768:772], axis=0).T
    out_out = one_sum[3].transpose(1, 0, 2).reshape(6, D)
    q_sum = one_sum[0].transpose(1, 0, 2).reshape(6, 2, 6, 1, HS)
    kv_sum = one_sum[1:3].transpose(2, 1, 0, 3).reshape(6, 2, 6, 2, HS)
    qkv_out = jnp.concatenate([q_sum, kv_sum], axis=3).reshape(6, 3 * D)

    return (
        layer_out,
        tokens_grad,
        vec_out[0],
        vec_out[1],
        vec_out[2],
        vec_out[3],
        qkv_out,
        out_out,
        up_out,
        down_out,
    )


def solution(mesh):
    fine = Mesh(mesh.devices.reshape(2, 4, 2, 4, 2), ALL)
    rows = P(ALL, None)
    vec = P(ALL)
    in_specs = (rows, vec, vec, vec, vec, rows, rows, rows, rows, rows)
    out_specs = (rows, rows, vec, vec, vec, vec, rows, rows, rows, rows)
    return jax.shard_map(local, mesh=fine, in_specs=in_specs, out_specs=out_specs, check_vma=False)
```
